768 devices in a mesh: clip: 16 (over z_lo, x), tile: 48 (over z_hi, y, core).
Axes of the slice: x: 4, y: 8, z: 12 (z_hi: 3, z_lo: 4; z = z_hi * 4 + z_lo), core: 2. Of those that a mesh axis runs over, the one named last changes fastest.
Arguments:
- clip_frames: bfloat16 [64, 96, 64, 128], P('clip', 'tile'), may hold values from -6 to 6
- conv_weight: bfloat16 [3, 3, 3, 128, 128], replicated, may hold values from -0.109375 to 0.109375
- conv_bias: float32 [128], replicated, may hold values from -3 to 3
- out_grad: bfloat16 [64, 96, 64, 128], P('clip', 'tile'), may hold values from -6 to 6
- prev_group: int32 [16], P('clip'), may hold values from -1 to 15, as said below
Outputs:
- conv_out: bfloat16 [64, 96, 64, 128], P('clip', 'tile')
- weight_grad: float32 [3, 3, 3, 128, 128], replicated
The draws below stay inside these ranges and needn't reach their ends.
Inputs may be any that keep to these rules, and one draw needn't show every extreme that they name: `prev_group`: no two groups name the same previous group, and following previous groups from any group ends at -1 after at most 16 steps.
All inputs are finite; a program needn't handle non-finite values.
Results may differ from the reference program's by a relative error of at most 0.0042.
Values may be sent and summed in bfloat16 or wider, within the bound.
A program may use at most 32 MiB of HBM per device.

```python
import math
import jax
import jax.numpy as jnp
from jax import lax

C = 128
FR = 4
TH = 2
W = 64
FRAMES = 64
H = 96
N_CLIP = 16
N_TILE = 48


def draw_prev_group(key, part):
    key_order = jax.random.fold_in(key, 11)
    key_start = jax.random.fold_in(key, 12)
    rest = jax.random.permutation(key_order, N_CLIP - 1).astype(jnp.int32)
    target = jnp.int32(N_CLIP // 2 - 1)
    spots = jnp.arange(N_CLIP - 1, dtype=jnp.int32)
    first_value = rest[0]
    rest = jnp.where(rest == target, first_value, rest)
    rest = jnp.where(spots == 0, target, rest)
    order = jnp.concatenate([jnp.array([N_CLIP - 1], jnp.int32), rest])
    starts = jax.random.randint(key_start, (N_CLIP,), 0, 3) == 0
    positions = jnp.arange(N_CLIP, dtype=jnp.int32)
    starts = jnp.where(positions == 0, True, jnp.where(positions == 1, False, starts))
    before = jnp.concatenate([jnp.array([-1], jnp.int32), order[:-1]])
    prev_at = jnp.where(starts, jnp.int32(-1), before)
    inverse = jnp.argsort(order, stable=True)
    return prev_at[inverse].astype(jnp.int32)


def steps_of(key, extent, split, low, high):
    factor_of, own = 1.0, jax.random.fold_in(key, 6)
    for axis_at, blocks in split:
        draws = jnp.exp(jax.random.uniform(jax.random.fold_in(own, axis_at), (blocks,), jnp.float32, low / len(split), high / len(split)))
        factor_of = factor_of * jnp.repeat(draws, extent[axis_at] // blocks).reshape([-1 if axis == axis_at else 1 for axis in range(len(extent))])
    return factor_of


def gaussian(key, extent, scale, most, shards=(), kind=jnp.bfloat16):
    loudness = steps_of(key, extent, shards, -0.22, 0.18) if shards else 1.0
    values = jax.random.normal(key, extent, jnp.float32) * scale * loudness
    return jnp.minimum(jnp.maximum(values, -most), most).astype(kind)


def setup_inputs(seed: int = 0) -> dict:
    seeds = jax.random.split(jax.random.key(seed), 6)
    clip_frames = gaussian(seeds[0], (FRAMES, H, W, C), 1.0, 6.0, ((0, 16), (1, 48)))
    conv_weight = gaussian(seeds[1], (3, 3, 3, C, C), (27 * C) ** -0.5, 0.109375)
    conv_bias = gaussian(seeds[2], (C,), 0.5, 3.0, (), jnp.float32)
    out_grad = gaussian(seeds[3], (FRAMES, H, W, C), 1.0, 6.0, ((0, 16), (1, 48)))
    prev_group = draw_prev_group(jax.random.fold_in(seeds[5], 71), 0)
    return {"clip_frames": clip_frames, "conv_weight": conv_weight, "conv_bias": conv_bias, "out_grad": out_grad, "prev_group": prev_group}


def window_columns(active, frame_tap, row_tap, group_frames, tall_rows, wide_cells):
    slab = active[frame_tap:frame_tap + group_frames, row_tap:row_tap + tall_rows]
    columns = jnp.concatenate([slab[:, :, shift_w:shift_w + wide_cells] for shift_w in range(3)], axis=-1)
    return columns.reshape(group_frames * tall_rows * wide_cells, columns.shape[-1])

def reference(clip_frames, conv_weight, conv_bias, out_grad, prev_group):
    tall_rows = TH * N_TILE
    wide_cells = W
    chans = conv_weight.shape[-1]
    weights = conv_weight.reshape(3, 3, 3 * chans, chans)
    factor = 1.0 / math.sqrt(FR * N_CLIP * tall_rows * wide_cells)

    def one_group(group_id):
        own_start = (group_id * FR).astype(jnp.int32)
        own_frames = lax.dynamic_slice_in_dim(clip_frames, own_start, FR, 0)
        grad_rows = lax.dynamic_slice_in_dim(out_grad, own_start, FR, 0).reshape(FR * tall_rows * wide_cells, chans)
        owner = prev_group[group_id]
        cache_start = (jnp.maximum(owner, 0) * FR + FR - 2).astype(jnp.int32)
        cached = lax.dynamic_slice_in_dim(clip_frames, cache_start, 2, 0)
        cached = jnp.where(owner >= 0, cached, jnp.zeros_like(cached))
        joined = jnp.concatenate([cached, own_frames], axis=0)
        joined = jnp.pad(joined, ((0, 0), (1, 1), (1, 1), (0, 0)))
        active = jax.nn.silu(joined.astype(jnp.float32)).astype(jnp.bfloat16)
        result = jnp.zeros((FR * tall_rows * wide_cells, chans), jnp.float32)
        grads = []
        for frame_tap in range(3):
            for row_tap in range(3):
                columns = window_columns(active, frame_tap, row_tap, FR, tall_rows, wide_cells)
                result = result + jnp.dot(columns, weights[frame_tap, row_tap], preferred_element_type=jnp.float32)
                grads.append(lax.dot_general(columns, grad_rows, (((0,), (0,)), ((), ())), preferred_element_type=jnp.float32))
        output = (result + conv_bias.astype(jnp.float32)).reshape(FR, tall_rows, wide_cells, chans).astype(jnp.bfloat16)
        return (output, jnp.stack(grads, axis=0))
    outputs, grad_terms = lax.map(one_group, jnp.arange(N_CLIP, dtype=jnp.int32))
    conv_out = outputs.reshape(N_CLIP * FR, tall_rows, wide_cells, chans)
    weight_grad = (lax.optimization_barrier(jnp.sum(grad_terms, axis=0)) * factor).reshape(3, 3, 3, chans, chans)
    return (conv_out, weight_grad)
```

```python
import functools
import math

import jax
import jax.numpy as jnp
from jax import lax
from jax.experimental import pallas as pl
from jax.experimental.pallas import tpu as pltpu
from jax.sharding import PartitionSpec as P

MESH = pl.DeviceIdType.MESH
NX, NZL, NZH, NY = 4, 4, 3, 8
NZ = NZH * NZL
F32, BF16 = jnp.float32, jnp.bfloat16


def sizes():
    half = 27 * 128 // 2
    part = half // NX
    slot = -(-part // (16 * NY)) * 16
    return half, part, slot


class Place:
    def __init__(self):
        clip, tile = lax.axis_index("clip"), lax.axis_index("tile")
        self.x, self.zl = clip % NX, clip // NX
        self.core, self.y, self.zh = tile % 2, (tile // 2) % NY, tile // (2 * NY)
        self.z = self.zh * NZL + self.zl
        self.clip, self.tile = clip, tile

    def at(self, x=None, y=None, z=None, core=None):
        x = self.x if x is None else x
        y = self.y if y is None else y
        z = self.z if z is None else z
        core = self.core if core is None else core
        return ((z % NZL) * NX + x, ((z // NZL) * NY + y) * 2 + core)


def kernel(
    factor, frames, weight, bias, grads, prev, out, gathered,
    act, cat, turned, gext, acc,
    ids_x, ids_z, gx, gm, gz, zx, zm, zz,
    local, core_out, core_in, sum_a, x_out, x_in, sum_b, y_out, y_in, z_buf,
    s_sem, r_sem,
):
    half, part, slot = sizes()
    me = Place()
    tiles = 2 * NY * NZH
    up, down = (me.tile + tiles - 1) % tiles, (me.tile + 1) % tiles
    other = 1 - me.core
    core_peer = me.at(core=other)
    diag_tile = jnp.where(me.core == 0, up, down)
    xs = [(me.x + j) % NX for j in range(1, NX)]
    ys = [(me.y + j) % NY for j in range(1, NY)]
    zs = [(me.z + j) % NZ for j in range(1, NZ)]
    zls = [(me.zl + j) % NZL for j in range(1, NZL)]
    x_peers = [me.at(x=x) for x in xs]
    y_peers = [me.at(y=y) for y in ys]
    z_peers = [me.at(z=z) for z in zs]
    zl_peers = [me.at(z=me.zh * NZL + zl) for zl in zls]

    barrier = pltpu.get_barrier_semaphore()
    everyone = [core_peer, (me.clip, diag_tile), *x_peers, *y_peers, *z_peers]
    for peer in everyone:
        pl.semaphore_signal(barrier, inc=1, device_id=peer, device_id_type=MESH)

    count = [0]
    started = []

    def send(src, dst, peer):
        k = count[0]
        count[0] += 1
        copy = pltpu.make_async_remote_copy(
            src_ref=src, dst_ref=dst, send_sem=s_sem.at[k], recv_sem=r_sem.at[k],
            device_id=peer, device_id_type=MESH,
        )
        copy.start()
        started.append(copy)
        return copy

    for s in range(4):
        v = frames[s].astype(F32)
        act[s, 1:3] = (v / (1.0 + jnp.exp(-v))).astype(BF16)
    own_id = jnp.full((8, 128), prev[0], jnp.int32)
    ids_x[me.x] = own_id
    ids_z[me.zl] = own_id
    gext[0:512] = grads[...].reshape(512, 128)
    pl.semaphore_wait(barrier, len(everyone))

    halo_up = send(act.at[:, 1], act.at[:, 3], (me.clip, up))
    halo_down = send(act.at[:, 2], act.at[:, 0], (me.clip, down))
    g_first = [send(gext.at[pl.ds(0, 256)], gx.at[me.x], peer) for peer in x_peers]
    id_x = [send(ids_x.at[me.x], ids_x.at[me.x], peer) for peer in x_peers]
    id_z = [send(ids_z.at[me.zl], ids_z.at[me.zl], peer) for peer in zl_peers]
    gx[me.x] = gext[0:256]

    halo_up.wait_recv()
    halo_down.wait_recv()
    top = jnp.where(me.tile == 0, 0.0, 1.0).astype(F32)
    bottom = jnp.where(me.tile == tiles - 1, 0.0, 1.0).astype(F32)

    row_at = lax.broadcasted_iota(jnp.int32, (64, 128), 0)

    def widen(s, _):
        for r in range(4):
            v = act[s, r].astype(F32)
            if r == 0:
                v = v * top
            if r == 3:
                v = v * bottom
            left = jnp.where(row_at == 0, 0.0, pltpu.roll(v, 1, 0))
            right = jnp.where(row_at == 63, 0.0, pltpu.roll(v, 63, 0))
            cat[s, r, :, 0:128] = left.astype(BF16)
            cat[s, r, :, 128:256] = v.astype(BF16)
            cat[s, r, :, 256:384] = right.astype(BF16)
        return 0

    lax.fori_loop(0, 4, widen, 0)

    def turn(s, b):
        for e in range(3):
            block = cat[s, pl.ds(b, 2), :, e * 128 : (e + 1) * 128].reshape(128, 128)
            start = pl.multiple_of((b * 3 + e) * 128, 128)
            turned[s, pl.ds(start, 128), :] = block.T

    for s in range(4):
        lax.fori_loop(0, 3, lambda b, _, s=s: (turn(s, b), 0)[1], 0)

    def grad_of(a):
        first = (2 - a) * 128

        def block(k, _):
            rows = pl.ds(pl.multiple_of(k * 384, 128), 384)
            total = jnp.zeros((384, 128), F32)
            for s in range(4):
                total = total + jnp.dot(
                    turned[s, rows, :], gext[first + s * 128 : first + (s + 1) * 128],
                    preferred_element_type=F32,
                )
            local[pl.ds(pl.multiple_of(a * 1152 + k * 384, 128), 384)] = total
            return 0

        lax.fori_loop(0, 3, block, 0)

    grad_of(2)

    for copy in g_first + id_x:
        copy.wait_recv()

    def pick(target, k):
        return (ids_x[k][0:1] == target * NX + me.x).astype(F32)

    def g_message(target):
        total = jnp.zeros((256, 128), F32)
        for k in range(NX):
            total = total + gx[k].astype(F32) * pick(target, k)
        return total.astype(BF16)

    g_second = []
    for j in range(1, NZL):
        gm[j] = g_message(zls[j - 1])
        g_second.append(send(gm.at[j], gz.at[j], zl_peers[j - 1]))
    gm[0] = g_message(me.zl)

    acc[...] = jnp.zeros((6, 128, 128), F32)

    def conv(a, _):
        for s in range(4):
            total = jnp.zeros((128, 128), F32)
            for b in range(3):
                total = total + jnp.dot(
                    cat[s, b : b + 2].reshape(128, 384), weight[a, b], preferred_element_type=F32
                )
            acc[s + 2 - a] = acc[s + 2 - a] + total
        return 0

    lax.fori_loop(0, 3, conv, 0)
    zx[me.x] = acc[4:6].reshape(256, 128).astype(BF16)
    z_first = [send(zx.at[me.x], zx.at[me.x], peer) for peer in x_peers]

    for copy in g_second:
        copy.wait_recv()
    gn = gm[0].astype(F32)
    for j in range(1, NZL):
        gn = gn + gz[j].astype(F32)
    gext[512:768] = gn.astype(BF16)
    grad_of(1)
    grad_of(0)

    start_other = pl.multiple_of(other * half, half)
    start_own = pl.multiple_of(me.core * half, half)
    core_out[...] = local[pl.ds(start_other, half)].astype(BF16)
    core_copy = send(core_out, core_in, core_peer)

    for copy in z_first + id_z:
        copy.wait_recv()

    def z_message(target):
        ids = ids_z[target][0:1]
        total = jnp.zeros((256, 128), F32)
        for k in range(NX):
            total = total + zx[k].astype(F32) * (ids == me.zl * NX + k).astype(F32)
        return total.astype(BF16)

    z_second = []
    for j in range(1, NZL):
        zm[j] = z_message(zls[j - 1])
        z_second.append(send(zm.at[j], zz.at[j], zl_peers[j - 1]))
    zm[0] = z_message(me.zl)

    core_copy.wait_recv()

    def add_core(k, _):
        rows = pl.ds(pl.multiple_of(k * part, 16), part)
        own = pl.ds(pl.multiple_of(start_own + k * part, 16), part)
        total = local[own] + core_in[rows].astype(F32)
        sum_a[rows] = total
        x_out[rows] = total.astype(BF16)
        return 0

    lax.fori_loop(0, NX, add_core, 0)

    x_copies = [
        send(x_out.at[pl.ds(pl.multiple_of(xs[j] * part, 16), part)], x_in.at[j], x_peers[j])
        for j in range(NX - 1)
    ]
    if NY * slot > part:
        y_out[pl.ds(part, NY * slot - part)] = jnp.zeros((NY * slot - part, 128), BF16)
        sum_b[pl.ds(part, NY * slot - part)] = jnp.zeros((NY * slot - part, 128), F32)
    for copy in x_copies:
        copy.wait_recv()
    total = sum_a[pl.ds(pl.multiple_of(me.x * part, 16), part)]
    for j in range(NX - 1):
        total = total + x_in[j].astype(F32)
    sum_b[0:part] = total
    y_out[0:part] = total.astype(BF16)

    y_copies = [
        send(y_out.at[pl.ds(pl.multiple_of(ys[j] * slot, 16), slot)], y_in.at[j], y_peers[j])
        for j in range(NY - 1)
    ]
    for copy in z_second:
        copy.wait_recv()
    zn = zm[0].astype(F32)
    for j in range(1, NZL):
        zn = zn + zz[j].astype(F32)
    acc[0:2] = acc[0:2] + zn.reshape(2, 128, 128)
    out[...] = (acc[0:4].reshape(512, 128) + bias[...]).astype(BF16).reshape(4, 2, 64, 128)

    for copy in y_copies:
        copy.wait_recv()
    total = sum_b[pl.ds(pl.multiple_of(me.y * slot, 16), slot)]
    for j in range(NY - 1):
        total = total + y_in[j].astype(F32)
    z_buf[me.z] = total.astype(BF16)

    z_copies = [send(z_buf.at[me.z], z_buf.at[me.z], peer) for peer in z_peers]
    for copy in z_copies:
        copy.wait_recv()
    total = z_buf[0].astype(F32)
    for k in range(1, NZ):
        total = total + z_buf[k].astype(F32)
    mine = pl.ds(pl.multiple_of(me.y * slot, 16), slot)
    gathered[me.core, me.x, mine] = (total * factor).astype(BF16)

    block = gathered.at[me.core, me.x, mine]
    for copy in [send(block, block, peer) for peer in y_peers]:
        copy.wait_recv()
    block = gathered.at[me.core, me.x]
    for copy in [send(block, block, peer) for peer in x_peers]:
        copy.wait_recv()
    block = gathered.at[me.core]
    send(block, block, core_peer).wait_recv()
    for copy in started:
        copy.wait_send()


def n_copies():
    return 2 + 5 * (NX - 1) + 3 * (NZL - 1) + 1 + 2 * (NY - 1) + (NZ - 1) + 1


def body(clip_frames, conv_weight, conv_bias, out_grad, prev_group):
    half, part, slot = sizes()
    factor = 1.0 / math.sqrt(
        4 * lax.axis_size("clip") * 2 * lax.axis_size("tile") * 64
    )
    vmem = pl.BlockSpec(memory_space=pltpu.VMEM)
    V = pltpu.VMEM
    n = n_copies()
    conv_out, gathered = pl.pallas_call(
        functools.partial(kernel, factor),
        out_shape=(
            jax.ShapeDtypeStruct((4, 2, 64, 128), BF16),
            jax.ShapeDtypeStruct((2, NX, NY * slot, 128), BF16),
        ),
        in_specs=[vmem, vmem, vmem, vmem, pl.BlockSpec(memory_space=pltpu.SMEM)],
        out_specs=(vmem, vmem),
        scratch_shapes=[
            V((4, 4, 64, 128), BF16),
            V((4, 4, 64, 384), BF16),
            V((4, 1152, 128), BF16),
            V((768, 128), BF16),
            V((6, 128, 128), F32),
            V((NX, 8, 128), jnp.int32),
            V((NZL, 8, 128), jnp.int32),
            V((NX, 256, 128), BF16),
            V((NZL, 256, 128), BF16),
            V((NZL, 256, 128), BF16),
            V((NX, 256, 128), BF16),
            V((NZL, 256, 128), BF16),
            V((NZL, 256, 128), BF16),
            V((3456, 128), F32),
            V((half, 128), BF16),
            V((half, 128), BF16),
            V((half, 128), F32),
            V((half, 128), BF16),
            V((NX - 1, part, 128), BF16),
            V((NY * slot, 128), F32),
            V((NY * slot, 128), BF16),
            V((NY - 1, slot, 128), BF16),
            V((NZ, slot, 128), BF16),
            pltpu.SemaphoreType.DMA((n,)),
            pltpu.SemaphoreType.DMA((n,)),
        ],
        compiler_params=pltpu.CompilerParams(
            collective_id=0, has_side_effects=True, vmem_limit_bytes=40 * 1024 * 1024
        ),
        name="conv_and_grad",
    )(
        clip_frames,
        conv_weight.reshape(3, 3, 384, 128),
        conv_bias.reshape(1, 128),
        out_grad,
        prev_group,
    )
    weight_grad = gathered[:, :, :part].astype(F32).reshape(3, 3, 3, 128, 128)
    return (conv_out, weight_grad)


def solution(mesh):
    return jax.shard_map(
        body,
        mesh=mesh,
        in_specs=(
            P("clip", "tile", None, None),
            P(),
            P(),
            P("clip", "tile", None, None),
            P("clip"),
        ),
        out_specs=(P("clip", "tile", None, None), P()),
        check_vma=False,
    )
```

```python
import functools
import math

import jax
import jax.numpy as jnp
from jax import lax
from jax.experimental import pallas as pl
from jax.experimental.pallas import tpu as pltpu
from jax.sharding import PartitionSpec as P

MESH = pl.DeviceIdType.MESH
NX, NZL, NZH, NY = 4, 4, 3, 8
NZ = NZH * NZL
F32, BF16 = jnp.float32, jnp.bfloat16


def sizes():
    half = 27 * 128 // 2
    part = half // NX
    slot = -(-part // (16 * NY)) * 16
    return half, part, slot


class Place:
    def __init__(self):
        clip, tile = lax.axis_index("clip"), lax.axis_index("tile")
        self.x, self.zl = clip % NX, clip // NX
        self.core, self.y, self.zh = tile % 2, (tile // 2) % NY, tile // (2 * NY)
        self.z = self.zh * NZL + self.zl
        self.clip, self.tile = clip, tile

    def at(self, x=None, y=None, z=None, core=None):
        x = self.x if x is None else x
        y = self.y if y is None else y
        z = self.z if z is None else z
        core = self.core if core is None else core
        return ((z % NZL) * NX + x, ((z // NZL) * NY + y) * 2 + core)


def kernel(
    factor, frames_hbm, weight_hbm, bias_hbm, grads_hbm, prev, out, gathered,
    frames, weight, bias, act, cat, turned, gext, acc,
    ids_x, ids_z, gx, gm, gz, zx, zm, zz,
    local, core_out, core_in, sum_a, x_out, x_in, y_out, y_in, z_buf,
    s_sem, r_sem, l_sem,
):
    half, part, slot = sizes()
    me = Place()
    tiles = 2 * NY * NZH
    up, down = (me.tile + tiles - 1) % tiles, (me.tile + 1) % tiles
    other = 1 - me.core
    core_peer = me.at(core=other)
    diag_tile = jnp.where(me.core == 0, up, down)
    pairs = NY // 2
    by_pair = sorted(range(pairs), key=lambda d: -min(d, pairs - d))
    my_pair, my_side = me.y // 2, me.y % 2
    sides = (my_side, 1 - my_side)
    by_z = sorted(range(1, NZ), key=lambda d: -min(d, NZ - d))
    xs = [(me.x + j) % NX for j in range(1, NX)]
    zls = [(me.zl + j) % NZL for j in range(1, NZL)]
    x_peers = [me.at(x=x) for x in xs]
    y_peer = {
        (d, r): me.at(y=(my_pair + d) % pairs * 2 + sides[r])
        for d in by_pair for r in range(2) if (d, r) != (0, 0)
    }
    z_peers = [me.at(z=(me.z + d) % NZ) for d in by_z]
    zl_peers = [me.at(z=me.zh * NZL + zl) for zl in zls]

    barrier = pltpu.get_barrier_semaphore()
    everyone = [core_peer, (me.clip, diag_tile), *x_peers, *y_peer.values(), *z_peers]
    for peer in everyone:
        pl.semaphore_signal(barrier, inc=1, device_id=peer, device_id_type=MESH)
    loads = [
        pltpu.make_async_copy(src, dst, l_sem.at[k])
        for k, (src, dst) in enumerate(
            ((frames_hbm, frames), (grads_hbm, gext.at[pl.ds(0, 512)]), (weight_hbm, weight), (bias_hbm, bias))
        )
    ]
    for load in loads:
        load.start()

    started = []

    def send(src, dst, peer):
        k = len(started)
        copy = pltpu.make_async_remote_copy(
            src_ref=src, dst_ref=dst, send_sem=s_sem.at[k], recv_sem=r_sem.at[k],
            device_id=peer, device_id_type=MESH,
        )
        copy.start()
        started.append(copy)
        return copy

    own_id = jnp.full((8, 128), prev[0], jnp.int32)
    ids_x[me.x] = own_id
    ids_z[me.zl] = own_id
    acc[...] = jnp.zeros((6, 128, 128), F32)
    pad = NY * slot - part
    if pad:
        core_out[:, part:] = jnp.zeros((NX, pad, 128), BF16)
        local[pl.ds(2 * half, pad)] = jnp.zeros((pad, 128), F32)
    loads[0].wait()
    for s in range(4):
        v = frames[s].astype(F32)
        act[s, 1:3] = (v / (1.0 + jnp.exp(-v))).astype(BF16)
    loads[1].wait()
    gx[me.x] = gext[0:256].reshape(2, 128, 128)
    pl.semaphore_wait(barrier, len(everyone))

    id_x = [send(ids_x.at[me.x], ids_x.at[me.x], peer) for peer in x_peers]
    g_first = [
        [send(gext.at[pl.ds(f * 128, 128)], gx.at[me.x, f], peer) for peer in x_peers]
        for f in range(2)
    ]
    halo_up = send(act.at[:, 1], act.at[:, 3], (me.clip, up))
    halo_down = send(act.at[:, 2], act.at[:, 0], (me.clip, down))
    id_z = [send(ids_z.at[me.zl], ids_z.at[me.zl], peer) for peer in zl_peers]

    for copy in id_x:
        copy.wait_recv()

    def g_message(target, f):
        total = jnp.zeros((128, 128), F32)
        for k in range(NX):
            chosen = (ids_x[k][0:1] == target * NX + me.x).astype(F32)
            total = total + gx[k, f].astype(F32) * chosen
        return total.astype(BF16)

    g_second = []
    for f in range(2):
        for copy in g_first[f]:
            copy.wait_recv()
        for j in range(NZL - 1):
            gm[j, f] = g_message(zls[j], f)
            g_second.append(send(gm.at[j, f], gz.at[j, f], zl_peers[j]))
    own_next = [g_message(me.zl, f).astype(F32) for f in range(2)]

    halo_up.wait_recv()
    halo_down.wait_recv()
    top = jnp.where(me.tile == 0, 0.0, 1.0).astype(F32)
    bottom = jnp.where(me.tile == tiles - 1, 0.0, 1.0).astype(F32)
    row_at = lax.broadcasted_iota(jnp.int32, (64, 128), 0)

    def widen(s, _):
        for r in range(4):
            v = act[s, r].astype(F32)
            if r == 0:
                v = v * top
            if r == 3:
                v = v * bottom
            left = jnp.where(row_at == 0, 0.0, pltpu.roll(v, 1, 0))
            right = jnp.where(row_at == 63, 0.0, pltpu.roll(v, 63, 0))
            cat[s, r, :, 0:128] = left.astype(BF16)
            cat[s, r, :, 128:256] = v.astype(BF16)
            cat[s, r, :, 256:384] = right.astype(BF16)
        return 0

    lax.fori_loop(0, 4, widen, 0)

    def turn(s, b):
        for e in range(3):
            block = cat[s, pl.ds(b, 2), :, e * 128 : (e + 1) * 128].reshape(128, 128)
            start = pl.multiple_of((b * 3 + e) * 128, 128)
            turned[s, pl.ds(start, 128), :] = block.T

    for s in range(4):
        lax.fori_loop(0, 3, lambda b, _, s=s: (turn(s, b), 0)[1], 0)

    def grad_of(a, frames_used, more):
        first = (2 - a) * 128

        def block(k, _):
            rows = pl.ds(pl.multiple_of(k * 384, 128), 384)
            at = pl.ds(pl.multiple_of(a * 1152 + k * 384, 128), 384)
            total = local[at] if more else jnp.zeros((384, 128), F32)
            for s in frames_used:
                total = total + jnp.dot(
                    turned[s, rows, :], gext[first + s * 128 : first + (s + 1) * 128],
                    preferred_element_type=F32,
                )
            local[at] = total
            return 0

        lax.fori_loop(0, 3, block, 0)

    grad_of(2, (0, 1, 2, 3), False)
    grad_of(1, (0, 1, 2), False)
    grad_of(0, (0, 1), False)

    loads[2].wait()
    loads[3].wait()

    def conv(a, _):
        for s in range(4):
            total = jnp.zeros((128, 128), F32)
            for b in range(3):
                total = total + jnp.dot(
                    cat[s, b : b + 2].reshape(128, 384), weight[a, b], preferred_element_type=F32
                )
            acc[s + 2 - a] = acc[s + 2 - a] + total
        return 0

    lax.fori_loop(0, 3, conv, 0)
    zx[me.x] = acc[4:6].reshape(256, 128).astype(BF16)
    z_first = [send(zx.at[me.x], zx.at[me.x], peer) for peer in x_peers]

    for copy in g_second:
        copy.wait_recv()
    for f in range(2):
        gn = own_next[f]
        for j in range(NZL - 1):
            gn = gn + gz[j, f].astype(F32)
        gext[512 + f * 128 : 640 + f * 128] = gn.astype(BF16)
    grad_of(1, (3,), True)
    grad_of(0, (2, 3), True)

    def pair_at(d):
        return pl.ds(pl.multiple_of((my_pair + d) % pairs * (2 * slot), 16), 2 * slot)

    def block_at(d, r):
        return pl.ds(
            pl.multiple_of(((my_pair + d) % pairs * 2 + sides[r]) * slot, 16), slot
        )

    for x in range(NX):
        core_out[x, 0:part] = local[
            pl.ds(pl.multiple_of(other * half + x * part, 16), part)
        ].astype(BF16)
    core_copies = []
    for d in by_pair:
        at = pair_at(d)
        core_copies.append(send(core_out.at[:, at], core_in.at[:, at], core_peer))

    x_copies = []
    for i, d in enumerate(by_pair):
        at = pair_at(d)
        core_copies[i].wait_recv()

        def both_cores(x):
            start = me.core * half + x * part + (my_pair + d) % pairs * (2 * slot)
            return local[pl.ds(pl.multiple_of(start, 16), 2 * slot)] + core_in[x, at].astype(F32)

        for j in range(NX - 1):
            x_out[j, at] = both_cores(xs[j]).astype(BF16)
        x_copies.append(
            [send(x_out.at[j, at], x_in.at[j, at], x_peers[j]) for j in range(NX - 1)]
        )
        sum_a[at] = both_cores(me.x)

    y_copies = {}
    for i, d in enumerate(by_pair):
        for copy in x_copies[i]:
            copy.wait_recv()
        for r in (1, 0):
            at = block_at(d, r)
            total = sum_a[at]
            for j in range(NX - 1):
                total = total + x_in[j, at].astype(F32)
            if (d, r) != (0, 0):
                k = 2 * d + r - 1
                y_out[k] = total.astype(BF16)
                y_copies[d, r] = send(y_out.at[k], y_in.at[k], y_peer[d, r])

    for copy in z_first + id_z:
        copy.wait_recv()

    def z_message(target):
        ids = ids_z[target][0:1]
        message = jnp.zeros((256, 128), F32)
        for k in range(NX):
            message = message + zx[k].astype(F32) * (ids == me.zl * NX + k).astype(F32)
        return message.astype(BF16)

    z_second = []
    for j in range(NZL - 1):
        zm[j] = z_message(zls[j])
        z_second.append(send(zm.at[j], zz.at[j], zl_peers[j]))
    zn = z_message(me.zl).astype(F32)

    for copy in y_copies.values():
        copy.wait_recv()
    for j in range(NY - 1):
        total = total + y_in[j].astype(F32)
    z_buf[me.z] = total.astype(BF16)

    z_copies = [send(z_buf.at[me.z], z_buf.at[me.z], peer) for peer in z_peers]

    for copy in z_second:
        copy.wait_recv()
    for j in range(NZL - 1):
        zn = zn + zz[j].astype(F32)
    acc[0:2] = acc[0:2] + zn.reshape(2, 128, 128)
    out[...] = (acc[0:4].reshape(512, 128) + bias[...]).astype(BF16).reshape(4, 2, 64, 128)

    for copy in z_copies:
        copy.wait_recv()
    total = z_buf[0].astype(F32)
    for k in range(1, NZ):
        total = total + z_buf[k].astype(F32)
    gathered[me.core, me.x, block_at(0, 0)] = (total * factor).astype(BF16)

    own = gathered.at[me.core, me.x, block_at(0, 0)]
    y_back = {key: send(own, own, y_peer[key]) for key in y_copies}
    x_back = []
    for d in reversed(by_pair):
        for r in range(2):
            if (d, r) != (0, 0):
                y_back[d, r].wait_recv()
        block = gathered.at[me.core, me.x, pair_at(pairs - d)]
        x_back.append([send(block, block, peer) for peer in x_peers])
    core_back = []
    for i, d in enumerate(reversed(by_pair)):
        for copy in x_back[i]:
            copy.wait_recv()
        block = gathered.at[me.core, :, pair_at(pairs - d)]
        core_back.append(send(block, block, core_peer))
    for copy in core_back:
        copy.wait_recv()
    for copy in started:
        copy.wait_send()


def n_copies():
    routing = 2 + 4 * (NX - 1) + 4 * (NZL - 1)
    scatter = NY // 2 + NY // 2 * (NX - 1) + (NY - 1)
    return routing + 2 * scatter + NZ - 1


def body(clip_frames, conv_weight, conv_bias, out_grad, prev_group):
    half, part, slot = sizes()
    factor = 1.0 / math.sqrt(
        4 * lax.axis_size("clip") * 2 * lax.axis_size("tile") * 64
    )
    hbm = pl.BlockSpec(memory_space=pltpu.HBM)
    V = pltpu.VMEM
    n = n_copies()
    conv_out, gathered = pl.pallas_call(
        functools.partial(kernel, factor),
        out_shape=(
            pltpu.VMEM((4, 2, 64, 128), BF16),
            pltpu.VMEM((2, NX, NY * slot, 128), BF16),
        ),
        in_specs=[hbm, hbm, hbm, hbm, pl.BlockSpec(memory_space=pltpu.SMEM)],
        out_specs=(pl.BlockSpec(memory_space=pltpu.VMEM),) * 2,
        scratch_shapes=[
            V((4, 2, 64, 128), BF16),
            V((3, 3, 384, 128), BF16),
            V((1, 128), F32),
            V((4, 4, 64, 128), BF16),
            V((4, 4, 64, 384), BF16),
            V((4, 1152, 128), BF16),
            V((768, 128), BF16),
            V((6, 128, 128), F32),
            V((NX, 8, 128), jnp.int32),
            V((NZL, 8, 128), jnp.int32),
            V((NX, 2, 128, 128), BF16),
            V((NZL, 2, 128, 128), BF16),
            V((NZL, 2, 128, 128), BF16),
            V((NX, 256, 128), BF16),
            V((NZL, 256, 128), BF16),
            V((NZL, 256, 128), BF16),
            V((2 * half - part + NY * slot, 128), F32),
            V((NX, NY * slot, 128), BF16),
            V((NX, NY * slot, 128), BF16),
            V((NY * slot, 128), F32),
            V((NX - 1, NY * slot, 128), BF16),
            V((NX - 1, NY * slot, 128), BF16),
            V((NY - 1, slot, 128), BF16),
            V((NY - 1, slot, 128), BF16),
            V((NZ, slot, 128), BF16),
            pltpu.SemaphoreType.DMA((n,)),
            pltpu.SemaphoreType.DMA((n,)),
            pltpu.SemaphoreType.DMA((7,)),
        ],
        compiler_params=pltpu.CompilerParams(
            collective_id=0, has_side_effects=True, vmem_limit_bytes=58000 * 1024
        ),
        name="conv_and_grad",
    )(
        clip_frames,
        conv_weight.reshape(3, 3, 384, 128),
        conv_bias.reshape(1, 128),
        out_grad.reshape(512, 128),
        prev_group,
    )
    weight_grad = gathered[:, :, :part].astype(F32).reshape(3, 3, 3, 128, 128)
    return (conv_out, weight_grad)


def solution(mesh):
    return jax.shard_map(
        body,
        mesh=mesh,
        in_specs=(
            P("clip", "tile", None, None),
            P(),
            P(),
            P("clip", "tile", None, None),
            P("clip"),
        ),
        out_specs=(P("clip", "tile", None, None), P()),
        check_vma=False,
    )
```

```python
import functools
import math

import jax
import jax.numpy as jnp
from jax import lax
from jax.experimental import pallas as pl
from jax.experimental.pallas import tpu as pltpu
from jax.sharding import PartitionSpec as P

MESH = pl.DeviceIdType.MESH
NX, NZL, NZH, NY = 4, 4, 3, 8
NZ = NZH * NZL
F32, BF16 = jnp.float32, jnp.bfloat16


def sizes():
    half = 27 * 128 // 2
    part = half // NX
    slot = -(-part // (16 * NY)) * 16
    return half, part, slot


class Place:
    def __init__(self):
        clip, tile = lax.axis_index("clip"), lax.axis_index("tile")
        self.x, self.zl = clip % NX, clip // NX
        self.core, self.y, self.zh = tile % 2, (tile // 2) % NY, tile // (2 * NY)
        self.z = self.zh * NZL + self.zl
        self.clip, self.tile = clip, tile

    def at(self, x=None, y=None, z=None, core=None):
        x = self.x if x is None else x
        y = self.y if y is None else y
        z = self.z if z is None else z
        core = self.core if core is None else core
        return ((z % NZL) * NX + x, ((z // NZL) * NY + y) * 2 + core)


def kernel(
    factor, frames_hbm, weight_hbm, bias_hbm, grads_hbm, prev, out, gathered,
    frames, weight, bias, act, cat, turned, gext, acc,
    ids_x, ids_z, gx, gm, gz, hz, hm, hx, zx, zm, zz,
    local, core_out, core_in, sum_a, x_out, x_in, y_out, y_in, z_buf,
    s_sem, r_sem, l_sem, round_1, round_2,
):
    half, part, slot = sizes()
    me = Place()
    tiles = 2 * NY * NZH
    up, down = (me.tile + tiles - 1) % tiles, (me.tile + 1) % tiles
    other = 1 - me.core
    core_peer = me.at(core=other)
    diag_tile = jnp.where(me.core == 0, up, down)
    pairs = NY // 2
    by_pair = sorted(range(pairs), key=lambda d: -min(d, pairs - d))
    my_pair, my_side = me.y // 2, me.y % 2
    sides = (my_side, 1 - my_side)
    by_z = sorted(range(1, NZ), key=lambda d: -min(d, NZ - d))
    xs = [(me.x + j) % NX for j in range(1, NX)]
    zls = [(me.zl + j) % NZL for j in range(1, NZL)]
    x_peers = [me.at(x=x) for x in xs]
    y_peer = {
        (d, r): me.at(y=(my_pair + d) % pairs * 2 + sides[r])
        for d in by_pair for r in range(2) if (d, r) != (0, 0)
    }
    z_peers = [me.at(z=(me.z + d) % NZ) for d in by_z]
    zl_peers = [me.at(z=me.zh * NZL + zl) for zl in zls]

    barrier = pltpu.get_barrier_semaphore()
    near = [core_peer, (me.clip, diag_tile), *x_peers, *zl_peers]
    near += [me.at(y=(me.y + d) % NY) for d in (1, NY - 1, 2, NY - 2) if d % NY]
    near += [me.at(z=(me.z + d) % NZ) for d in (1, NZ - 1, 2, NZ - 2) if d % NZ]
    for peer in near:
        pl.semaphore_signal(barrier, inc=1, device_id=peer, device_id_type=MESH)
    loads = [
        pltpu.make_async_copy(src, dst, l_sem.at[k])
        for k, (src, dst) in enumerate(
            ((frames_hbm, frames), (grads_hbm, gext.at[pl.ds(0, 512)]), (weight_hbm, weight), (bias_hbm, bias))
        )
    ]
    for load in loads:
        load.start()

    started = []

    def send(src, dst, peer):
        k = len(started)
        copy = pltpu.make_async_remote_copy(
            src_ref=src, dst_ref=dst, send_sem=s_sem.at[k], recv_sem=r_sem.at[k],
            device_id=peer, device_id_type=MESH,
        )
        copy.start()
        started.append(copy)
        return copy

    own_id = jnp.full((8, 128), prev[0], jnp.int32)
    ids_x[me.x] = own_id
    ids_z[me.zl] = own_id
    acc[...] = jnp.zeros((6, 128, 128), F32)
    pad = NY * slot - part
    if pad:
        core_out[:, part:] = jnp.zeros((NX, pad, 128), BF16)
        local[pl.ds(2 * half, pad)] = jnp.zeros((pad, 128), F32)
    loads[0].wait()
    row_at = lax.broadcasted_iota(jnp.int32, (64, 128), 0)

    def widen(s, r, v):
        left = jnp.where(row_at == 0, 0.0, pltpu.roll(v, 1, 0))
        right = jnp.where(row_at == 63, 0.0, pltpu.roll(v, 63, 0))
        cat[s, r, :, 0:128] = left.astype(BF16)
        cat[s, r, :, 128:256] = v.astype(BF16)
        cat[s, r, :, 256:384] = right.astype(BF16)

    def turn(s, b):
        for e in range(3):
            block = cat[s, b : b + 2, :, e * 128 : (e + 1) * 128].reshape(128, 128)
            start = (b * 3 + e) * 128
            turned[s, start : start + 128, :] = block.T

    def activate(s, _):
        for r in (1, 2):
            v = frames[s, r - 1].astype(F32)
            active = (v / (1.0 + jnp.exp(-v))).astype(BF16)
            act[s, r] = active
            widen(s, r, active.astype(F32))
        turn(s, 1)
        return 0

    lax.fori_loop(0, 4, activate, 0)
    loads[1].wait()
    gx[me.x] = gext[0:128]
    hz[me.zl] = gext[128:256]
    pl.semaphore_wait(barrier, len(near))
    for peer in near:
        pl.semaphore_signal(round_1, inc=1, device_id=peer, device_id_type=MESH)

    id_x = [send(ids_x.at[me.x], ids_x.at[me.x], peer) for peer in x_peers]
    id_z = [send(ids_z.at[me.zl], ids_z.at[me.zl], peer) for peer in zl_peers]
    g_first = [send(gext.at[pl.ds(0, 128)], gx.at[me.x], peer) for peer in x_peers]
    h_first = [send(gext.at[pl.ds(128, 128)], hz.at[me.zl], peer) for peer in zl_peers]
    halo_up = send(act.at[:, 1], act.at[:, 3], (me.clip, up))
    halo_down = send(act.at[:, 2], act.at[:, 0], (me.clip, down))

    def chosen(items, ids, target, number):
        message = jnp.zeros(items.shape[1:], F32)
        for k in range(number):
            message = message + items[k].astype(F32) * (ids[k][0:1] == target).astype(F32)
        return message.astype(BF16)

    for copy in id_x + g_first:
        copy.wait_recv()
    g_second = []
    for j in range(NZL - 1):
        gm[j] = chosen(gx, ids_x, zls[j] * NX + me.x, NX)
        g_second.append(send(gm.at[j], gz.at[j], zl_peers[j]))
    pl.semaphore_wait(round_1, len(near))
    for peer in near:
        pl.semaphore_signal(round_2, inc=1, device_id=peer, device_id_type=MESH)
    for copy in id_z + h_first:
        copy.wait_recv()
    h_second = []
    for j in range(NX - 1):
        hm[j] = chosen(hz, ids_z, me.zl * NX + xs[j], NZL)
        h_second.append(send(hm.at[j], hx.at[j], x_peers[j]))
    own_next = [
        chosen(items, ids, me.clip, number).astype(F32)
        for items, ids, number in ((gx, ids_x, NX), (hz, ids_z, NZL))
    ]

    halo_up.wait_recv()
    halo_down.wait_recv()
    top = jnp.where(me.tile == 0, 0.0, 1.0).astype(F32)
    bottom = jnp.where(me.tile == tiles - 1, 0.0, 1.0).astype(F32)

    def widen_halo(s, _):
        widen(s, 0, act[s, 0].astype(F32) * top)
        widen(s, 3, act[s, 3].astype(F32) * bottom)
        return 0

    lax.fori_loop(0, 4, widen_halo, 0)
    lax.fori_loop(0, 4, lambda s, _: (turn(s, 0), turn(s, 2), 0)[2], 0)

    def grad_of(a, frames_used, more):
        first = (2 - a) * 128

        def block(k, _):
            rows = pl.ds(pl.multiple_of(k * 384, 128), 384)
            at = pl.ds(pl.multiple_of(a * 1152 + k * 384, 128), 384)
            total = local[at] if more else jnp.zeros((384, 128), F32)
            for s in frames_used:
                total = total + jnp.dot(
                    turned[s, rows, :], gext[first + s * 128 : first + (s + 1) * 128],
                    preferred_element_type=F32,
                )
            local[at] = total
            return 0

        lax.fori_loop(0, 3, block, 0)

    grad_of(2, (0, 1, 2, 3), False)
    grad_of(1, (0, 1, 2), False)
    grad_of(0, (0, 1), False)

    for copy in g_second + h_second:
        copy.wait_recv()
    for f, pieces, number in ((0, gz, NZL), (1, hx, NX)):
        gn = own_next[f]
        for j in range(number - 1):
            gn = gn + pieces[j].astype(F32)
        gext[512 + f * 128 : 640 + f * 128] = gn.astype(BF16)
    grad_of(1, (3,), True)
    grad_of(0, (2, 3), True)

    def pair_at(d):
        return pl.ds(pl.multiple_of((my_pair + d) % pairs * (2 * slot), 16), 2 * slot)

    def block_at(d, r):
        return pl.ds(
            pl.multiple_of(((my_pair + d) % pairs * 2 + sides[r]) * slot, 16), slot
        )

    for x in range(NX):
        core_out[x, 0:part] = local[
            pl.ds(pl.multiple_of(other * half + x * part, 16), part)
        ].astype(BF16)
    core_copies = []
    for d in by_pair:
        at = pair_at(d)
        core_copies.append(send(core_out.at[:, at], core_in.at[:, at], core_peer))

    x_copies = []
    for i, d in enumerate(by_pair):
        at = pair_at(d)
        core_copies[i].wait_recv()

        def both_cores(x):
            start = me.core * half + x * part + (my_pair + d) % pairs * (2 * slot)
            return local[pl.ds(pl.multiple_of(start, 16), 2 * slot)] + core_in[x, at].astype(F32)

        for j in range(NX - 1):
            x_out[j, at] = both_cores(xs[j]).astype(BF16)
        x_copies.append(
            [send(x_out.at[j, at], x_in.at[j, at], x_peers[j]) for j in range(NX - 1)]
        )
        sum_a[at] = both_cores(me.x)

    pl.semaphore_wait(round_2, len(near))
    y_copies = {}
    for i, d in enumerate(by_pair):
        for copy in x_copies[i]:
            copy.wait_recv()
        for r in (1, 0):
            at = block_at(d, r)
            total = sum_a[at]
            for j in range(NX - 1):
                total = total + x_in[j, at].astype(F32)
            if (d, r) != (0, 0):
                k = 2 * d + r - 1
                y_out[k] = total.astype(BF16)
                y_copies[d, r] = send(y_out.at[k], y_in.at[k], y_peer[d, r])

    loads[2].wait()
    loads[3].wait()

    def conv(a, _):
        for s in range(4):
            total = jnp.zeros((128, 128), F32)
            for b in range(3):
                total = total + jnp.dot(
                    cat[s, b : b + 2].reshape(128, 384), weight[a, b], preferred_element_type=F32
                )
            acc[s + 2 - a] = acc[s + 2 - a] + total
        return 0

    lax.fori_loop(0, 3, conv, 0)
    zx[me.x] = acc[4:6].reshape(256, 128).astype(BF16)
    z_first = [send(zx.at[me.x], zx.at[me.x], peer) for peer in x_peers]

    for copy in y_copies.values():
        copy.wait_recv()
    for j in range(NY - 1):
        total = total + y_in[j].astype(F32)
    z_buf[me.z] = total.astype(BF16)

    z_copies = [send(z_buf.at[me.z], z_buf.at[me.z], peer) for peer in z_peers]

    for copy in z_first:
        copy.wait_recv()

    def z_message(target):
        ids = ids_z[target][0:1]
        message = jnp.zeros((256, 128), F32)
        for k in range(NX):
            message = message + zx[k].astype(F32) * (ids == me.zl * NX + k).astype(F32)
        return message.astype(BF16)

    for j in range(NZL - 1):
        zm[j] = z_message(zls[j])
    zn = z_message(me.zl).astype(F32)

    for copy in z_copies:
        copy.wait_recv()
    total = z_buf[0].astype(F32)
    for k in range(1, NZ):
        total = total + z_buf[k].astype(F32)
    gathered[me.core, me.x, block_at(0, 0)] = (total * factor).astype(BF16)

    own = gathered.at[me.core, me.x, block_at(0, 0)]
    y_back = {key: send(own, own, y_peer[key]) for key in y_copies}
    z_second = [send(zm.at[j], zz.at[j], zl_peers[j]) for j in range(NZL - 1)]
    x_back = []
    for d in reversed(by_pair):
        for r in range(2):
            if (d, r) != (0, 0):
                y_back[d, r].wait_recv()
        block = gathered.at[me.core, me.x, pair_at(pairs - d)]
        x_back.append([send(block, block, peer) for peer in x_peers])
    for copy in z_second:
        copy.wait_recv()
    for j in range(NZL - 1):
        zn = zn + zz[j].astype(F32)
    acc[0:2] = acc[0:2] + zn.reshape(2, 128, 128)
    out[...] = (acc[0:4].reshape(512, 128) + bias[...]).astype(BF16).reshape(4, 2, 64, 128)

    core_back = []
    for i, d in enumerate(reversed(by_pair)):
        for copy in x_back[i]:
            copy.wait_recv()
        block = gathered.at[me.core, :, pair_at(pairs - d)]
        core_back.append(send(block, block, core_peer))
    for copy in core_back:
        copy.wait_recv()
    for copy in started:
        copy.wait_send()


def n_copies():
    routing = 2 + 4 * (NX - 1) + 4 * (NZL - 1)
    scatter = NY // 2 + NY // 2 * (NX - 1) + (NY - 1)
    return routing + 2 * scatter + NZ - 1


def body(clip_frames, conv_weight, conv_bias, out_grad, prev_group):
    half, part, slot = sizes()
    factor = 1.0 / math.sqrt(
        4 * lax.axis_size("clip") * 2 * lax.axis_size("tile") * 64
    )
    hbm = pl.BlockSpec(memory_space=pltpu.HBM)
    V = pltpu.VMEM
    n = n_copies()
    conv_out, gathered = pl.pallas_call(
        functools.partial(kernel, factor),
        out_shape=(
            pltpu.VMEM((4, 2, 64, 128), BF16),
            pltpu.VMEM((2, NX, NY * slot, 128), BF16),
        ),
        in_specs=[hbm, hbm, hbm, hbm, pl.BlockSpec(memory_space=pltpu.SMEM)],
        out_specs=(pl.BlockSpec(memory_space=pltpu.VMEM),) * 2,
        scratch_shapes=[
            V((4, 2, 64, 128), BF16),
            V((3, 3, 384, 128), BF16),
            V((1, 128), F32),
            V((4, 4, 64, 128), BF16),
            V((4, 4, 64, 384), BF16),
            V((4, 1152, 128), BF16),
            V((768, 128), BF16),
            V((6, 128, 128), F32),
            V((NX, 8, 128), jnp.int32),
            V((NZL, 8, 128), jnp.int32),
            V((NX, 128, 128), BF16),
            V((NZL, 128, 128), BF16),
            V((NZL, 128, 128), BF16),
            V((NZL, 128, 128), BF16),
            V((NX, 128, 128), BF16),
            V((NX, 128, 128), BF16),
            V((NX, 256, 128), BF16),
            V((NZL, 256, 128), BF16),
            V((NZL, 256, 128), BF16),
            V((2 * half - part + NY * slot, 128), F32),
            V((NX, NY * slot, 128), BF16),
            V((NX, NY * slot, 128), BF16),
            V((NY * slot, 128), F32),
            V((NX - 1, NY * slot, 128), BF16),
            V((NX - 1, NY * slot, 128), BF16),
            V((NY - 1, slot, 128), BF16),
            V((NY - 1, slot, 128), BF16),
            V((NZ, slot, 128), BF16),
            pltpu.SemaphoreType.DMA((n,)),
            pltpu.SemaphoreType.DMA((n,)),
            pltpu.SemaphoreType.DMA((7,)),
            pltpu.SemaphoreType.REGULAR,
            pltpu.SemaphoreType.REGULAR,
        ],
        compiler_params=pltpu.CompilerParams(
            collective_id=0, has_side_effects=True, vmem_limit_bytes=58000 * 1024
        ),
        name="conv_and_grad",
    )(
        clip_frames,
        conv_weight.reshape(3, 3, 384, 128),
        conv_bias.reshape(1, 128),
        out_grad.reshape(512, 128),
        prev_group,
    )
    weight_grad = gathered[:, :, :part].astype(F32).reshape(3, 3, 3, 128, 128)
    return (conv_out, weight_grad)


def solution(mesh):
    return jax.shard_map(
        body,
        mesh=mesh,
        in_specs=(
            P("clip", "tile", None, None),
            P(),
            P(),
            P("clip", "tile", None, None),
            P("clip"),
        ),
        out_specs=(P("clip", "tile", None, None), P()),
        check_vma=False,
    )
```

```python
import functools
import math

import jax
import jax.numpy as jnp
from jax import lax
from jax.experimental import pallas as pl
from jax.experimental.pallas import tpu as pltpu
from jax.sharding import PartitionSpec as P

MESH = pl.DeviceIdType.MESH
NX, NZL, NZH, NY = 4, 4, 3, 8
NZ = NZH * NZL
F32, BF16 = jnp.float32, jnp.bfloat16


def sizes():
    half = 27 * 128 // 2
    part = half // NX
    slot = -(-part // (16 * NY)) * 16
    return half, part, slot


class Place:
    def __init__(self):
        clip, tile = lax.axis_index("clip"), lax.axis_index("tile")
        self.x, self.zl = clip % NX, clip // NX
        self.core, self.y, self.zh = tile % 2, (tile // 2) % NY, tile // (2 * NY)
        self.z = self.zh * NZL + self.zl
        self.clip, self.tile = clip, tile

    def at(self, x=None, y=None, z=None, core=None):
        x = self.x if x is None else x
        y = self.y if y is None else y
        z = self.z if z is None else z
        core = self.core if core is None else core
        return ((z % NZL) * NX + x, ((z // NZL) * NY + y) * 2 + core)


class Either:
    def __init__(self, first, when_first, when_not):
        self.first, self.when_first, self.when_not = first, when_first, when_not

    def both(self, act):
        pl.when(self.first)(lambda: act(self.when_first))
        pl.when(jnp.logical_not(self.first))(lambda: act(self.when_not))

    def start(self):
        self.both(lambda copy: copy.start())

    def wait_recv(self):
        self.both(lambda copy: copy.wait_recv())

    def wait_send(self):
        self.both(lambda copy: copy.wait_send())


def kernel(
    factor, frames_hbm, weight_hbm, bias_hbm, grads_hbm, prev, out, gathered,
    frames, weight, bias, act, cat, turned, gext, acc,
    ids_x, ids_z, gx, gm, gz, hz, hm, hx, zx, zm, zz,
    local, core_out, core_in, sum_a, x_out, x_in, y_out, y_in, z_buf,
    s_sem, r_sem, l_sem, round_1, round_2,
):
    half, part, slot = sizes()
    me = Place()
    tiles = 2 * NY * NZH
    up, down = (me.tile + tiles - 1) % tiles, (me.tile + 1) % tiles
    other = 1 - me.core
    core_peer = me.at(core=other)
    diag_tile = jnp.where(me.core == 0, up, down)
    pairs = NY // 2
    by_pair = sorted(range(pairs), key=lambda d: -min(d, pairs - d))
    my_pair, my_side = me.y // 2, me.y % 2
    sides = (my_side, 1 - my_side)
    by_z = sorted(range(1, NZ), key=lambda d: -min(d, NZ - d))
    by_x = sorted(range(1, NX), key=lambda d: -min(d, NX - d))
    xs = [(me.x + d) % NX for d in by_x]
    zls = [(me.zl + j) % NZL for j in range(1, NZL)]
    x_peers = [me.at(x=x) for x in xs]
    y_peer = {
        (d, r): me.at(y=(my_pair + d) % pairs * 2 + sides[r])
        for d in by_pair for r in range(2) if (d, r) != (0, 0)
    }
    z_peers = [me.at(z=(me.z + d) % NZ) for d in by_z]
    zl_peers = [me.at(z=me.zh * NZL + zl) for zl in zls]

    barrier = pltpu.get_barrier_semaphore()
    near = [core_peer, (me.clip, diag_tile), *x_peers, *zl_peers]
    near += [me.at(y=(me.y + d) % NY) for d in (1, NY - 1, 2, NY - 2) if d % NY]
    near += [me.at(z=(me.z + d) % NZ) for d in (1, NZ - 1, 2, NZ - 2) if d % NZ]
    for peer in near:
        pl.semaphore_signal(barrier, inc=1, device_id=peer, device_id_type=MESH)
    loads = [
        pltpu.make_async_copy(src, dst, l_sem.at[k])
        for k, (src, dst) in enumerate(
            ((frames_hbm, frames), (grads_hbm, gext.at[pl.ds(0, 512)]), (weight_hbm, weight), (bias_hbm, bias))
        )
    ]
    for load in loads:
        load.start()

    started = []
    sent = [0]

    def send(src, dst, peer):
        k = len(started)
        copy = pltpu.make_async_remote_copy(
            src_ref=src, dst_ref=dst, send_sem=s_sem.at[k], recv_sem=r_sem.at[k],
            device_id=peer, device_id_type=MESH,
        )
        copy.start()
        started.append(copy)
        return copy

    def send_pair(src_of, dst_of, d, peer):
        k = len(started)
        pair = (my_pair + d) % pairs
        copies = []
        for rows in (part - (pairs - 1) * 2 * slot, 2 * slot):
            at = pl.ds(pl.multiple_of(pair * (2 * slot), 16), rows)
            copies.append(
                pltpu.make_async_remote_copy(
                    src_ref=src_of(at), dst_ref=dst_of(at), send_sem=s_sem.at[k],
                    recv_sem=r_sem.at[k], device_id=peer, device_id_type=MESH,
                )
            )
        copy = Either(pair == pairs - 1, *copies)
        copy.start()
        started.append(copy)
        return copy

    def wait_sent(count):
        for copy in started[sent[0] : count]:
            copy.wait_send()
        sent[0] = count

    own_id = jnp.full((8, 128), prev[0], jnp.int32)
    ids_x[me.x] = own_id
    ids_z[me.zl] = own_id
    acc[...] = jnp.zeros((6, 128, 128), F32)
    pad = NY * slot - part
    if pad:
        core_in[:, part:] = jnp.zeros((NX, pad, 128), BF16)
        x_in[:, part:] = jnp.zeros((NX - 1, pad, 128), BF16)
        local[pl.ds(2 * half, pad)] = jnp.zeros((pad, 128), F32)
    loads[0].wait()
    row_at = lax.broadcasted_iota(jnp.int32, (64, 128), 0)

    def widen(s, r, v):
        left = jnp.where(row_at == 0, 0.0, pltpu.roll(v, 1, 0))
        right = jnp.where(row_at == 63, 0.0, pltpu.roll(v, 63, 0))
        cat[s, r, :, 0:128] = left.astype(BF16)
        cat[s, r, :, 128:256] = v.astype(BF16)
        cat[s, r, :, 256:384] = right.astype(BF16)

    def turn(s, b):
        for e in range(3):
            block = cat[s, b : b + 2, :, e * 128 : (e + 1) * 128].reshape(128, 128)
            start = (b * 3 + e) * 128
            turned[s, start : start + 128, :] = block.T

    def activate(s, _):
        for r in (1, 2):
            v = frames[s, r - 1].astype(F32)
            active = (v / (1.0 + jnp.exp(-v))).astype(BF16)
            act[s, r] = active
            widen(s, r, active.astype(F32))
        turn(s, 1)
        return 0

    lax.fori_loop(0, 4, activate, 0)
    loads[1].wait()
    gx[me.x] = gext[0:128]
    hz[me.zl] = gext[128:256]
    pl.semaphore_wait(barrier, len(near))
    for peer in near:
        pl.semaphore_signal(round_1, inc=1, device_id=peer, device_id_type=MESH)

    id_x = [send(ids_x.at[me.x], ids_x.at[me.x], peer) for peer in x_peers]
    id_z = [send(ids_z.at[me.zl], ids_z.at[me.zl], peer) for peer in zl_peers]
    g_first = [send(gext.at[pl.ds(0, 128)], gx.at[me.x], peer) for peer in x_peers]
    h_first = [send(gext.at[pl.ds(128, 128)], hz.at[me.zl], peer) for peer in zl_peers]
    halo_up = send(act.at[:, 1], act.at[:, 3], (me.clip, up))
    halo_down = send(act.at[:, 2], act.at[:, 0], (me.clip, down))

    def chosen(items, ids, target, number):
        message = jnp.zeros(items.shape[1:], F32)
        for k in range(number):
            message = message + items[k].astype(F32) * (ids[k][0:1] == target).astype(F32)
        return message.astype(BF16)

    for copy in id_x + g_first:
        copy.wait_recv()
    g_second = []
    for j in range(NZL - 1):
        gm[j] = chosen(gx, ids_x, zls[j] * NX + me.x, NX)
        g_second.append(send(gm.at[j], gz.at[j], zl_peers[j]))
    pl.semaphore_wait(round_1, len(near))
    for peer in near:
        pl.semaphore_signal(round_2, inc=1, device_id=peer, device_id_type=MESH)
    for copy in id_z + h_first:
        copy.wait_recv()
    h_second = []
    for j in range(NX - 1):
        hm[j] = chosen(hz, ids_z, me.zl * NX + xs[j], NZL)
        h_second.append(send(hm.at[j], hx.at[j], x_peers[j]))
    own_next = [
        chosen(items, ids, me.clip, number).astype(F32)
        for items, ids, number in ((gx, ids_x, NX), (hz, ids_z, NZL))
    ]

    halo_up.wait_recv()
    halo_down.wait_recv()
    top = jnp.where(me.tile == 0, 0.0, 1.0).astype(F32)
    bottom = jnp.where(me.tile == tiles - 1, 0.0, 1.0).astype(F32)

    def widen_halo(s, _):
        widen(s, 0, act[s, 0].astype(F32) * top)
        widen(s, 3, act[s, 3].astype(F32) * bottom)
        return 0

    lax.fori_loop(0, 4, widen_halo, 0)
    lax.fori_loop(0, 4, lambda s, _: (turn(s, 0), turn(s, 2), 0)[2], 0)

    def grad_of(a, frames_used, more):
        first = (2 - a) * 128

        def block(k, _):
            rows = pl.ds(pl.multiple_of(k * 384, 128), 384)
            at = pl.ds(pl.multiple_of(a * 1152 + k * 384, 128), 384)
            total = local[at] if more else jnp.zeros((384, 128), F32)
            for s in frames_used:
                total = total + jnp.dot(
                    turned[s, rows, :], gext[first + s * 128 : first + (s + 1) * 128],
                    preferred_element_type=F32,
                )
            local[at] = total
            return 0

        lax.fori_loop(0, 3, block, 0)

    grad_of(2, (0, 1, 2, 3), False)
    grad_of(1, (0, 1, 2), False)
    grad_of(0, (0, 1), False)

    for copy in g_second + h_second:
        copy.wait_recv()
    for f, pieces, number in ((0, gz, NZL), (1, hx, NX)):
        gn = own_next[f]
        for j in range(number - 1):
            gn = gn + pieces[j].astype(F32)
        gext[512 + f * 128 : 640 + f * 128] = gn.astype(BF16)
    grad_of(1, (3,), True)
    grad_of(0, (2, 3), True)

    def pair_at(d):
        return pl.ds(pl.multiple_of((my_pair + d) % pairs * (2 * slot), 16), 2 * slot)

    def block_at(d, r):
        return pl.ds(
            pl.multiple_of(((my_pair + d) % pairs * 2 + sides[r]) * slot, 16), slot
        )

    for x in range(NX):
        core_out[x, 0:part] = local[
            pl.ds(pl.multiple_of(other * half + x * part, 16), part)
        ].astype(BF16)
    core_copies = []
    for d in by_pair:
        core_copies.append(
            send_pair(lambda at: core_out.at[:, at], lambda at: core_in.at[:, at], d, core_peer)
        )

    x_copies = []
    for i, d in enumerate(by_pair):
        at = pair_at(d)
        core_copies[i].wait_recv()

        def both_cores(x):
            start = me.core * half + x * part + (my_pair + d) % pairs * (2 * slot)
            return local[pl.ds(pl.multiple_of(start, 16), 2 * slot)] + core_in[x, at].astype(F32)

        for j in range(NX - 1):
            x_out[j, at] = both_cores(xs[j]).astype(BF16)
        x_copies.append(
            [
                send_pair(
                    lambda at, j=j: x_out.at[j, at], lambda at, j=j: x_in.at[j, at], d, x_peers[j]
                )
                for j in range(NX - 1)
            ]
        )
        sum_a[at] = both_cores(me.x)

    pl.semaphore_wait(round_2, len(near))
    y_copies = {}
    for i, d in enumerate(by_pair):
        for copy in x_copies[i]:
            copy.wait_recv()
        for r in (1, 0):
            at = block_at(d, r)
            total = sum_a[at]
            for j in range(NX - 1):
                total = total + x_in[j, at].astype(F32)
            if (d, r) != (0, 0):
                k = 2 * d + r - 1
                y_out[k] = total.astype(BF16)
                y_copies[d, r] = send(y_out.at[k], y_in.at[k], y_peer[d, r])

    loads[2].wait()
    loads[3].wait()

    def conv(a, _):
        for s in range(4):
            total = jnp.zeros((128, 128), F32)
            for b in range(3):
                total = total + jnp.dot(
                    cat[s, b : b + 2].reshape(128, 384), weight[a, b], preferred_element_type=F32
                )
            acc[s + 2 - a] = acc[s + 2 - a] + total
        return 0

    lax.fori_loop(0, 3, conv, 0)
    zx[me.x] = acc[4:6].reshape(256, 128).astype(BF16)
    z_first = [send(zx.at[me.x], zx.at[me.x], peer) for peer in x_peers]

    for copy in y_copies.values():
        copy.wait_recv()
    for j in range(NY - 1):
        total = total + y_in[j].astype(F32)
    z_buf[me.z] = total.astype(BF16)

    before_z = len(started)
    z_copies = [send(z_buf.at[me.z], z_buf.at[me.z], peer) for peer in z_peers]

    for copy in z_first:
        copy.wait_recv()

    def z_message(target):
        ids = ids_z[target][0:1]
        message = jnp.zeros((256, 128), F32)
        for k in range(NX):
            message = message + zx[k].astype(F32) * (ids == me.zl * NX + k).astype(F32)
        return message.astype(BF16)

    for j in range(NZL - 1):
        zm[j] = z_message(zls[j])
    zn = z_message(me.zl).astype(F32)

    wait_sent(before_z)
    for copy in z_copies:
        copy.wait_recv()
    total = z_buf[0].astype(F32)
    for k in range(1, NZ):
        total = total + z_buf[k].astype(F32)
    gathered[me.core, me.x, block_at(0, 0)] = (total * factor).astype(BF16)

    own = gathered.at[me.core, me.x, block_at(0, 0)]
    y_back = {key: send(own, own, y_peer[key]) for key in y_copies}
    z_second = [send(zm.at[j], zz.at[j], zl_peers[j]) for j in range(NZL - 1)]
    x_back = []
    for d in reversed(by_pair):
        for r in range(2):
            if (d, r) != (0, 0):
                y_back[d, r].wait_recv()
        def block_of(at):
            return gathered.at[me.core, me.x, at]

        x_back.append([send_pair(block_of, block_of, pairs - d, peer) for peer in x_peers])
    for copy in z_second:
        copy.wait_recv()
    for j in range(NZL - 1):
        zn = zn + zz[j].astype(F32)
    acc[0:2] = acc[0:2] + zn.reshape(2, 128, 128)
    out[...] = (acc[0:4].reshape(512, 128) + bias[...]).astype(BF16).reshape(4, 2, 64, 128)

    core_back = []
    for i, d in enumerate(reversed(by_pair)):
        for copy in x_back[i]:
            copy.wait_recv()
        def side_of(at):
            return gathered.at[me.core, :, at]

        core_back.append(send_pair(side_of, side_of, pairs - d, core_peer))
    wait_sent(len(started) - len(core_back))
    for copy in core_back:
        copy.wait_recv()
    wait_sent(len(started))


def widen_result(conv, gathered, conv_hbm, grad_hbm, wide, sem):
    part = wide.shape[2]
    copies = [pltpu.make_async_copy(conv, conv_hbm, sem.at[2 * NX])]
    copies[0].start()
    for core in range(2):
        for x in range(NX):
            wide[core, x] = gathered[core, x, 0:part].astype(F32)
            copy = pltpu.make_async_copy(
                wide.at[core, x], grad_hbm.at[core, x], sem.at[core * NX + x]
            )
            copy.start()
            copies.append(copy)
    for copy in copies:
        copy.wait()


def n_copies():
    routing = 2 + 4 * (NX - 1) + 4 * (NZL - 1)
    scatter = NY // 2 + NY // 2 * (NX - 1) + (NY - 1)
    return routing + 2 * scatter + NZ - 1


def body(clip_frames, conv_weight, conv_bias, out_grad, prev_group):
    half, part, slot = sizes()
    factor = 1.0 / math.sqrt(
        4 * lax.axis_size("clip") * 2 * lax.axis_size("tile") * 64
    )
    hbm = pl.BlockSpec(memory_space=pltpu.HBM)
    V = pltpu.VMEM
    n = n_copies()
    conv_out, gathered = pl.pallas_call(
        functools.partial(kernel, factor),
        out_shape=(
            pltpu.VMEM((4, 2, 64, 128), BF16),
            pltpu.VMEM((2, NX, NY * slot, 128), BF16),
        ),
        in_specs=[hbm, hbm, hbm, hbm, pl.BlockSpec(memory_space=pltpu.SMEM)],
        out_specs=(pl.BlockSpec(memory_space=pltpu.VMEM),) * 2,
        scratch_shapes=[
            V((4, 2, 64, 128), BF16),
            V((3, 3, 384, 128), BF16),
            V((1, 128), F32),
            V((4, 4, 64, 128), BF16),
            V((4, 4, 64, 384), BF16),
            V((4, 1152, 128), BF16),
            V((768, 128), BF16),
            V((6, 128, 128), F32),
            V((NX, 8, 128), jnp.int32),
            V((NZL, 8, 128), jnp.int32),
            V((NX, 128, 128), BF16),
            V((NZL, 128, 128), BF16),
            V((NZL, 128, 128), BF16),
            V((NZL, 128, 128), BF16),
            V((NX, 128, 128), BF16),
            V((NX, 128, 128), BF16),
            V((NX, 256, 128), BF16),
            V((NZL, 256, 128), BF16),
            V((NZL, 256, 128), BF16),
            V((2 * half - part + NY * slot, 128), F32),
            V((NX, NY * slot, 128), BF16),
            V((NX, NY * slot, 128), BF16),
            V((NY * slot, 128), F32),
            V((NX - 1, NY * slot, 128), BF16),
            V((NX - 1, NY * slot, 128), BF16),
            V((NY - 1, slot, 128), BF16),
            V((NY - 1, slot, 128), BF16),
            V((NZ, slot, 128), BF16),
            pltpu.SemaphoreType.DMA((n,)),
            pltpu.SemaphoreType.DMA((n,)),
            pltpu.SemaphoreType.DMA((7,)),
            pltpu.SemaphoreType.REGULAR,
            pltpu.SemaphoreType.REGULAR,
        ],
        compiler_params=pltpu.CompilerParams(
            collective_id=0, has_side_effects=True, vmem_limit_bytes=58000 * 1024
        ),
        name="conv_and_grad",
    )(
        clip_frames,
        conv_weight.reshape(3, 3, 384, 128),
        conv_bias.reshape(1, 128),
        out_grad.reshape(512, 128),
        prev_group,
    )
    vmem = pl.BlockSpec(memory_space=pltpu.VMEM)
    conv_out, weight_grad = pl.pallas_call(
        widen_result,
        out_shape=(
            jax.ShapeDtypeStruct((4, 2, 64, 128), BF16),
            jax.ShapeDtypeStruct((2, NX, part, 128), F32),
        ),
        in_specs=[vmem, vmem],
        out_specs=(hbm, hbm),
        scratch_shapes=[
            V((2, NX, part, 128), F32),
            pltpu.SemaphoreType.DMA((2 * NX + 1,)),
        ],
        compiler_params=pltpu.CompilerParams(vmem_limit_bytes=16 * 1024 * 1024),
        name="widen_result",
    )(conv_out, gathered)
    return (conv_out, weight_grad.reshape(3, 3, 3, 128, 128))


def solution(mesh):
    return jax.shard_map(
        body,
        mesh=mesh,
        in_specs=(
            P("clip", "tile", None, None),
            P(),
            P(),
            P("clip", "tile", None, None),
            P("clip"),
        ),
        out_specs=(P("clip", "tile", None, None), P()),
        check_vma=False,
    )
```
